32 devices in a mesh: req: 2 (over y), patch: 16 (over z, x, core).
Axes of the slice: x: 2, y: 2, z: 4, core: 2. Of those that a mesh axis runs over, the one named last changes fastest.
Arguments:
- queries: bfloat16 [768, 2560], P(('req', 'patch')), parts along dimension 0, may hold values from -200 to 200, as said below
- stale_kv: bfloat16 [2, 768, 2560], P(None, ('req', 'patch')), parts along dimension 1, may hold values from -6 to 6, as said below
- residual_codes: int32 [2, 768, 2560], P(None, ('req', 'patch')), parts along dimension 1, may hold values from 0 to 255
- scale_exponents: int32 [2, 768, 80], P(None, ('req', 'patch')), parts along dimension 1, may hold values from 6 to 9
Outputs:
- attended: bfloat16 [768, 2560], P(('req', 'patch')), parts along dimension 0
The draws below stay inside these ranges and needn't reach their ends.
There are 2 independent parts, one for each index of `req`. The reference program is written for one: setup_inputs(seed, part) draws one part's arguments, and reference() takes and returns one part's arrays. A program takes and returns all parts, laid end to end along the dimension named above; each array names one. Nothing has to cross between parts.
Inputs may be any that keep to these rules, and one draw needn't show every extreme that they name: `queries`: queries are of order three; a few rows may be far larger. `stale_kv`: keys and values of last step, of order one.
All inputs are finite; a program needn't handle non-finite values.
Results may differ from the reference program's by a relative error of at most 0.0073.
Values may be sent and summed in bfloat16 or wider, within the bound.
A program may use at most 128 MiB of HBM per device.

```python
import jax
import jax.numpy as jnp
from jax import lax

HEADS = 20
HD = 128
BLOCK = 32
TOKENS = 384


def shared_keys(key):
    return jnp.clip(jax.random.normal(key, (2, TOKENS, HEADS * HD), jnp.float32), -6.0, 6.0)


def draw_stale_kv(key, part):
    base = shared_keys(key)
    return base.astype(jnp.bfloat16)


def draw_queries(key, part):
    key = jax.random.fold_in(key, 7)
    drawn = 3.0 * jnp.clip(jax.random.normal(key, (TOKENS, HEADS * HD), jnp.float32), -4.0, 4.0)
    return drawn.astype(jnp.bfloat16)


def set_ends(values, rng, low, largest):
    spot = [jax.random.randint(jax.random.fold_in(rng, axis), (), 0, length) for axis, length in enumerate(values.shape)]
    widest = values.shape.index(max(values.shape))
    neighbour = spot[:widest] + [(spot[widest] + 1) % values.shape[widest]] + spot[widest + 1:]
    return values.at[tuple(spot)].set(low).at[tuple(neighbour)].set(largest)


def setup_inputs(seed: int = 0, part: int = 0) -> dict:
    key_of = jax.random.split(jax.random.key(seed), 5)
    own_keys = jax.random.split(jax.random.fold_in(key_of[4], part), 5)
    return {
        "queries": draw_queries(jax.random.fold_in(jax.random.fold_in(key_of[4], part), 71), part),
        "stale_kv": draw_stale_kv(jax.random.fold_in(jax.random.fold_in(key_of[4], part), 71), part),
        "residual_codes": set_ends(jax.random.randint(own_keys[2], (2, TOKENS, HEADS * HD), 0, 256), jax.random.fold_in(own_keys[2], 1), 0, 255).astype(jnp.int32),
        "scale_exponents": set_ends(jax.random.randint(own_keys[3], (2, TOKENS, HEADS * HD // BLOCK), 6, 10), jax.random.fold_in(own_keys[3], 1), 6, 9).astype(jnp.int32),
    }


def decode_residual(residual_codes, scale_exponents, width):
    sign_part = 1.0 - 2.0 * (residual_codes // 128).astype(jnp.float32)
    exponent = (residual_codes // 8) % 16
    mantissa = (residual_codes % 8).astype(jnp.float32)
    power = jnp.exp2((exponent - 7).astype(jnp.float32))
    normal_value = (1.0 + mantissa / 8.0) * power
    small_value = mantissa / 8.0 * (2.0 ** -6)
    magnitude = jnp.where(exponent == 0, small_value, normal_value)
    block_scale = jnp.exp2((scale_exponents - 16).astype(jnp.float32))
    shaped = (sign_part * magnitude).reshape(scale_exponents.shape + (width,))
    return (shaped * block_scale[..., None]).reshape(residual_codes.shape)


def head_attention(operands):
    head_query, head_key, head_value = operands
    score_scale = HD ** -0.5
    scores = jnp.dot(head_query, head_key.T, preferred_element_type=jnp.float32) * score_scale
    top_score = jnp.max(scores, axis=1, keepdims=True)
    weights_exp = jnp.exp(scores - top_score)
    total = jnp.sum(weights_exp, axis=1, keepdims=True)
    summed = jnp.dot(weights_exp.astype(jnp.bfloat16), head_value, preferred_element_type=jnp.float32)
    return (summed / total).astype(jnp.bfloat16)


def reference(queries, stale_kv, residual_codes, scale_exponents):
    residual = decode_residual(residual_codes, scale_exponents, BLOCK)
    rebuilt = (stale_kv.astype(jnp.float32) + residual).astype(jnp.bfloat16)
    head_query = queries.reshape(TOKENS, HEADS, HD).transpose(1, 0, 2)
    head_key = rebuilt[0].reshape(TOKENS, HEADS, HD).transpose(1, 0, 2)
    head_value = rebuilt[1].reshape(TOKENS, HEADS, HD).transpose(1, 0, 2)
    outputs = lax.map(head_attention, (head_query, head_key, head_value))
    return outputs.transpose(1, 0, 2).reshape(TOKENS, HEADS * HD)
```

```python
import functools
import math

import jax
import jax.numpy as jnp
from jax import lax
from jax.experimental import pallas as pl
from jax.experimental.pallas import tpu as pltpu
from jax.sharding import PartitionSpec as P

HEADS = 20
HD = 128
BLOCK = 32
MESH = pl.DeviceIdType.MESH


def spans(n):
    return max((HEADS * d + HEADS - 1) // n - HEADS * d // n + 1 for d in range(n))


def kernel(
    n, group, span,
    q_ref, stale_ref, codes_ref, scale_ref, out_ref,
    stale_v, codes_v, scale_v, own, kv_in, q_in, o_buf,
    in_sem, kv_send, kv_recv, q_send, q_recv, o_send, o_recv,
):
    per = HEADS // group
    blocks = n // group
    rows = q_ref.shape[0]
    req = lax.axis_index("req")
    me = lax.axis_index("patch")
    my_blk, my_pos = lax.div(me, group), lax.rem(me, group)

    def first_head(d):
        return jnp.minimum(lax.div(HEADS * d, n), HEADS - span)

    barrier = pltpu.get_barrier_semaphore()

    def greet(k, c):
        pl.semaphore_signal(
            barrier, inc=1, device_id=(req, lax.rem(me + k, n)), device_id_type=MESH
        )
        return c

    loads = [
        pltpu.make_async_copy(scale_ref, scale_v, in_sem.at[0]),
        pltpu.make_async_copy(codes_ref, codes_v, in_sem.at[1]),
        pltpu.make_async_copy(stale_ref, stale_v, in_sem.at[2]),
    ]
    for load in loads:
        load.start()
    lax.fori_loop(1, n, greet, 0)
    for load in loads:
        load.wait()

    spread = (
        lax.shift_right_logical(
            lax.broadcasted_iota(jnp.int32, (HEADS * HD // BLOCK, HEADS * HD), 1), 5
        )
        == lax.broadcasted_iota(jnp.int32, (HEADS * HD // BLOCK, HEADS * HD), 0)
    ).astype(jnp.float32).astype(jnp.bfloat16)
    for x in range(2):
        power = lax.shift_left(jnp.ones_like(scale_v[x]), scale_v[x])
        power = power.astype(jnp.float32).astype(jnp.bfloat16)
        block_scale = jnp.dot(power, spread, preferred_element_type=jnp.float32)
        for h in range(HEADS):
            lanes = slice(h * HD, (h + 1) * HD)
            code = codes_v[x, :, lanes]
            exponent = lax.shift_right_logical(code, 3) & 15
            mantissa = code & 7
            whole = jnp.where(exponent > 0, mantissa + 8, mantissa)
            whole = lax.shift_left(whole, jnp.maximum(exponent - 1, 0))
            whole = jnp.where(code >= 128, -whole, whole)
            residual = whole.astype(jnp.float32) * (block_scale[:, lanes] * 2.0**-25)
            kept = stale_v[x, :, lanes].astype(jnp.float32)
            own[h, x] = (kept + residual).astype(jnp.bfloat16)

    pl.semaphore_wait(barrier, n - 1)

    def kv_copy(d):
        return pltpu.make_async_remote_copy(
            src_ref=own.at[pl.ds(first_head(d), span)],
            dst_ref=kv_in.at[:, :, me],
            send_sem=kv_send.at[d],
            recv_sem=kv_recv.at[me],
            device_id=(req, d),
            device_id_type=MESH,
        )

    def send_kv(k, c):
        kv_copy(lax.rem(me + k, n)).start()
        return c

    own_kv = pltpu.make_async_copy(
        own.at[pl.ds(first_head(me), span)], kv_in.at[:, :, me], kv_recv.at[me]
    )

    def q_route(h):
        unit = h * blocks + my_blk
        d = lax.div(unit, per)
        return d, lax.rem(unit, per) * group + my_pos

    def q_lanes(ref, h):
        return ref.at[:, pl.ds(pl.multiple_of(h * HD, HD), HD)]

    def q_copy(h):
        d, slot = q_route(h)
        return pltpu.make_async_remote_copy(
            src_ref=q_lanes(q_ref, h), dst_ref=q_in.at[slot],
            send_sem=q_send.at[h], recv_sem=q_recv.at[slot],
            device_id=(req, d), device_id_type=MESH,
        )

    def q_local(h):
        d, slot = q_route(h)
        return pltpu.make_async_copy(q_lanes(q_ref, h), q_in.at[slot], q_recv.at[slot])

    def send_q(h, c):
        d, slot = q_route(h)

        @pl.when(d != me)
        def _():
            q_copy(h).start()

        @pl.when(d == me)
        def _():
            q_local(h).start()

        return c

    lax.fori_loop(0, HEADS, send_q, 0)
    lax.fori_loop(1, n, send_kv, 0)
    own_kv.start()

    def wait_q(slot, c):
        pltpu.make_async_copy(q_lanes(q_ref, 0), q_in.at[slot], q_recv.at[slot]).wait()
        return c

    def wait_kv(s, c):
        pltpu.make_async_copy(
            own.at[pl.ds(0, span)], kv_in.at[:, :, s], kv_recv.at[s]
        ).wait()
        return c

    lax.fori_loop(0, HEADS, wait_q, 0)
    lax.fori_loop(0, n, wait_kv, 0)

    def o_route(slot):
        t, i = divmod(slot, group)
        unit = me * per + t
        h = lax.div(unit, blocks)
        return h, lax.rem(unit, blocks) * group + i

    for t in range(per):
        h = lax.div(me * per + t, blocks)
        at = h - first_head(me)
        head_query = q_in[t * group:(t + 1) * group].astype(jnp.float32)
        head_query = head_query.reshape(group * rows, HD).astype(jnp.bfloat16)
        head_key = kv_in[at, 0].astype(jnp.float32).reshape(n * rows, HD).astype(jnp.bfloat16)
        head_value = kv_in[at, 1].astype(jnp.float32).reshape(n * rows, HD).astype(jnp.bfloat16)
        scores = lax.dot_general(
            head_query, head_key, (((1,), (1,)), ((), ())),
            preferred_element_type=jnp.float32,
        ) * (HD ** -0.5)
        weights = jnp.exp(scores - jnp.max(scores, axis=1, keepdims=True))
        total = jnp.sum(weights, axis=1, keepdims=True)
        summed = jnp.dot(
            weights.astype(jnp.bfloat16), head_value, preferred_element_type=jnp.float32
        )
        o_buf[t * group:(t + 1) * group] = (
            (summed / total).reshape(group, rows, HD).astype(jnp.bfloat16)
        )
        for i in range(group):
            slot = t * group + i
            h, d = o_route(slot)

            @pl.when(d != me)
            def _():
                pltpu.make_async_remote_copy(
                    src_ref=o_buf.at[slot], dst_ref=q_lanes(out_ref, h),
                    send_sem=o_send.at[slot], recv_sem=o_recv.at[h],
                    device_id=(req, d), device_id_type=MESH,
                ).start()

            @pl.when(d == me)
            def _():
                pltpu.make_async_copy(
                    o_buf.at[slot], q_lanes(out_ref, h), o_recv.at[h]
                ).start()

    def drain_kv(k, c):
        kv_copy(lax.rem(me + k, n)).wait_send()
        return c

    def drain_q(h, c):
        d, slot = q_route(h)

        @pl.when(d != me)
        def _():
            q_copy(h).wait_send()

        return c

    lax.fori_loop(1, n, drain_kv, 0)
    lax.fori_loop(0, HEADS, drain_q, 0)
    for slot in range(HEADS):
        h, d = o_route(slot)

        @pl.when(d != me)
        def _():
            pltpu.make_async_remote_copy(
                src_ref=o_buf.at[slot], dst_ref=q_lanes(out_ref, h),
                send_sem=o_send.at[slot], recv_sem=o_recv.at[h],
                device_id=(req, d), device_id_type=MESH,
            ).wait_send()

    def wait_o(h, c):
        pltpu.make_async_copy(o_buf.at[0], q_lanes(out_ref, h), o_recv.at[h]).wait()
        return c

    lax.fori_loop(0, HEADS, wait_o, 0)


def solution(mesh):
    n = mesh.shape["patch"]
    group = math.gcd(HEADS, n)
    span = spans(n)

    def per_device(queries, stale_kv, residual_codes, scale_exponents):
        rows = queries.shape[0]
        anywhere = pl.BlockSpec(memory_space=pl.ANY)
        bf16, dma = jnp.bfloat16, pltpu.SemaphoreType.DMA
        return pl.pallas_call(
            functools.partial(kernel, n, group, span),
            out_shape=jax.ShapeDtypeStruct(queries.shape, bf16),
            in_specs=[anywhere] * 4,
            out_specs=anywhere,
            scratch_shapes=[
                pltpu.VMEM(stale_kv.shape, bf16),
                pltpu.VMEM(residual_codes.shape, jnp.int32),
                pltpu.VMEM(scale_exponents.shape, jnp.int32),
                pltpu.VMEM((HEADS, 2, rows, HD), bf16),
                pltpu.VMEM((span, 2, n, rows, HD), bf16),
                pltpu.VMEM((HEADS, rows, HD), bf16),
                pltpu.VMEM((HEADS, rows, HD), bf16),
                dma((3,)),
                dma((n,)), dma((n,)),
                dma((HEADS,)), dma((HEADS,)),
                dma((HEADS,)), dma((HEADS,)),
            ],
            compiler_params=pltpu.CompilerParams(
                collective_id=0, has_side_effects=True, vmem_limit_bytes=48 << 20
            ),
        )(queries, stale_kv, residual_codes, scale_exponents)

    return jax.shard_map(
        per_device,
        mesh=mesh,
        in_specs=(
            P(("req", "patch"), None),
            P(None, ("req", "patch"), None),
            P(None, ("req", "patch"), None),
            P(None, ("req", "patch"), None),
        ),
        out_specs=P(("req", "patch"), None),
        check_vma=False,
    )
```

```python
import functools
import math

import jax
import jax.numpy as jnp
from jax import lax
from jax.experimental import pallas as pl
from jax.experimental.pallas import tpu as pltpu
from jax.sharding import PartitionSpec as P

HEADS = 20
HD = 128
BLOCK = 32
MESH = pl.DeviceIdType.MESH


def spans(n):
    return max((HEADS * d + HEADS - 1) // n - HEADS * d // n + 1 for d in range(n))


def kernel(
    n, group, span,
    q_ref, stale_ref, codes_ref, scale_ref, out_ref,
    stale_v, codes_v, scale_v, own, kv_in, q_in, o_buf,
    in_sem, kv_send, kv_recv, q_send, q_recv, o_send, o_recv,
):
    per = HEADS // group
    blocks = n // group
    rows = q_ref.shape[0]
    req = lax.axis_index("req")
    me = lax.axis_index("patch")
    my_blk, my_pos = lax.div(me, group), lax.rem(me, group)

    def first_head(d):
        return jnp.minimum(lax.div(HEADS * d, n), HEADS - span)

    barrier = pltpu.get_barrier_semaphore()

    def greet(k, c):
        pl.semaphore_signal(
            barrier, inc=1, device_id=(req, lax.rem(me + k, n)), device_id_type=MESH
        )
        return c

    loads = [
        pltpu.make_async_copy(scale_ref, scale_v, in_sem.at[0]),
        pltpu.make_async_copy(codes_ref, codes_v, in_sem.at[1]),
        pltpu.make_async_copy(stale_ref, stale_v, in_sem.at[2]),
    ]
    for load in loads:
        load.start()
    lax.fori_loop(1, n, greet, 0)
    for load in loads:
        load.wait()

    spread = (
        lax.shift_right_logical(
            lax.broadcasted_iota(jnp.int32, (HEADS * HD // BLOCK, HEADS * HD), 1), 5
        )
        == lax.broadcasted_iota(jnp.int32, (HEADS * HD // BLOCK, HEADS * HD), 0)
    ).astype(jnp.float32).astype(jnp.bfloat16)
    for x in range(2):
        power = lax.shift_left(jnp.ones_like(scale_v[x]), scale_v[x])
        power = power.astype(jnp.float32).astype(jnp.bfloat16)
        block_scale = jnp.dot(power, spread, preferred_element_type=jnp.float32)
        for h in range(HEADS):
            lanes = slice(h * HD, (h + 1) * HD)
            code = codes_v[x, :, lanes]
            exponent = lax.shift_right_logical(code, 3) & 15
            mantissa = code & 7
            whole = jnp.where(exponent > 0, mantissa + 8, mantissa)
            whole = lax.shift_left(whole, jnp.maximum(exponent - 1, 0))
            whole = jnp.where(code >= 128, -whole, whole)
            residual = whole.astype(jnp.float32) * (block_scale[:, lanes] * 2.0**-25)
            kept = stale_v[x, :, lanes].astype(jnp.float32)
            own[h, x] = (kept + residual).astype(jnp.bfloat16)

    pl.semaphore_wait(barrier, n - 1)

    def kv_copy(d):
        return pltpu.make_async_remote_copy(
            src_ref=own.at[pl.ds(first_head(d), span)],
            dst_ref=kv_in.at[:, :, me],
            send_sem=kv_send.at[d],
            recv_sem=kv_recv.at[me],
            device_id=(req, d),
            device_id_type=MESH,
        )

    def send_kv(k, c):
        kv_copy(lax.rem(me + k, n)).start()
        return c

    own_kv = pltpu.make_async_copy(
        own.at[pl.ds(first_head(me), span)], kv_in.at[:, :, me], kv_recv.at[me]
    )

    def q_route(h):
        unit = h * blocks + my_blk
        d = lax.div(unit, per)
        return d, lax.rem(unit, per) * group + my_pos

    def q_lanes(ref, h):
        return ref.at[:, pl.ds(pl.multiple_of(h * HD, HD), HD)]

    def q_copy(h):
        d, slot = q_route(h)
        return pltpu.make_async_remote_copy(
            src_ref=q_lanes(q_ref, h), dst_ref=q_in.at[slot],
            send_sem=q_send.at[h], recv_sem=q_recv.at[slot],
            device_id=(req, d), device_id_type=MESH,
        )

    def q_local(h):
        d, slot = q_route(h)
        return pltpu.make_async_copy(q_lanes(q_ref, h), q_in.at[slot], q_recv.at[slot])

    def send_q(h, c):
        d, slot = q_route(h)

        @pl.when(d != me)
        def _():
            q_copy(h).start()

        @pl.when(d == me)
        def _():
            q_local(h).start()

        return c

    lax.fori_loop(0, HEADS, send_q, 0)
    lax.fori_loop(1, n, send_kv, 0)
    own_kv.start()

    def wait_q(slot, c):
        pltpu.make_async_copy(q_lanes(q_ref, 0), q_in.at[slot], q_recv.at[slot]).wait()
        return c

    def wait_kv(s, c):
        pltpu.make_async_copy(
            own.at[pl.ds(0, span)], kv_in.at[:, :, s], kv_recv.at[s]
        ).wait()
        return c

    lax.fori_loop(0, HEADS, wait_q, 0)
    lax.fori_loop(0, n, wait_kv, 0)

    def o_route(slot):
        t, i = divmod(slot, group)
        unit = me * per + t
        h = lax.div(unit, blocks)
        return h, lax.rem(unit, blocks) * group + i

    for t in range(per):
        h = lax.div(me * per + t, blocks)
        at = h - first_head(me)
        head_query = q_in[t * group:(t + 1) * group].astype(jnp.float32)
        head_query = head_query.reshape(group * rows, HD).astype(jnp.bfloat16)
        head_key = kv_in[at, 0].astype(jnp.float32).reshape(n * rows, HD).astype(jnp.bfloat16)
        head_value = kv_in[at, 1].astype(jnp.float32).reshape(n * rows, HD).astype(jnp.bfloat16)
        scores = lax.dot_general(
            head_query, head_key, (((1,), (1,)), ((), ())),
            preferred_element_type=jnp.float32,
        ) * (HD ** -0.5)
        weights = jnp.exp(scores - jnp.max(scores, axis=1, keepdims=True))
        total = jnp.sum(weights, axis=1, keepdims=True)
        summed = jnp.dot(
            weights.astype(jnp.bfloat16), head_value, preferred_element_type=jnp.float32
        )
        o_buf[t * group:(t + 1) * group] = (
            (summed / total).reshape(group, rows, HD).astype(jnp.bfloat16)
        )
        for i in range(group):
            slot = t * group + i
            h, d = o_route(slot)

            @pl.when(d != me)
            def _():
                pltpu.make_async_remote_copy(
                    src_ref=o_buf.at[slot], dst_ref=q_lanes(out_ref, h),
                    send_sem=o_send.at[slot], recv_sem=o_recv.at[h],
                    device_id=(req, d), device_id_type=MESH,
                ).start()

            @pl.when(d == me)
            def _():
                pltpu.make_async_copy(
                    o_buf.at[slot], q_lanes(out_ref, h), o_recv.at[h]
                ).start()

    def drain_kv(k, c):
        kv_copy(lax.rem(me + k, n)).wait_send()
        return c

    def drain_q(h, c):
        d, slot = q_route(h)

        @pl.when(d != me)
        def _():
            q_copy(h).wait_send()

        return c

    lax.fori_loop(1, n, drain_kv, 0)
    lax.fori_loop(0, HEADS, drain_q, 0)
    for slot in range(HEADS):
        h, d = o_route(slot)

        @pl.when(d != me)
        def _():
            pltpu.make_async_remote_copy(
                src_ref=o_buf.at[slot], dst_ref=q_lanes(out_ref, h),
                send_sem=o_send.at[slot], recv_sem=o_recv.at[h],
                device_id=(req, d), device_id_type=MESH,
            ).wait_send()

    def wait_o(h, c):
        pltpu.make_async_copy(o_buf.at[0], q_lanes(out_ref, h), o_recv.at[h]).wait()
        return c

    lax.fori_loop(0, HEADS, wait_o, 0)


def solution(mesh):
    n = mesh.shape["patch"]
    group = math.gcd(HEADS, n)
    span = spans(n)

    def per_device(queries, stale_kv, residual_codes, scale_exponents):
        rows = queries.shape[0]
        far = pl.BlockSpec(memory_space=pltpu.HBM)
        bf16, dma = jnp.bfloat16, pltpu.SemaphoreType.DMA
        return pl.pallas_call(
            functools.partial(kernel, n, group, span),
            out_shape=jax.ShapeDtypeStruct(queries.shape, bf16),
            in_specs=[far] * 4,
            out_specs=pl.BlockSpec(memory_space=pl.ANY),
            scratch_shapes=[
                pltpu.VMEM(stale_kv.shape, bf16),
                pltpu.VMEM(residual_codes.shape, jnp.int32),
                pltpu.VMEM(scale_exponents.shape, jnp.int32),
                pltpu.VMEM((HEADS, 2, rows, HD), bf16),
                pltpu.VMEM((span, 2, n, rows, HD), bf16),
                pltpu.VMEM((HEADS, rows, HD), bf16),
                pltpu.VMEM((HEADS, rows, HD), bf16),
                dma((3,)),
                dma((n,)), dma((n,)),
                dma((HEADS,)), dma((HEADS,)),
                dma((HEADS,)), dma((HEADS,)),
            ],
            compiler_params=pltpu.CompilerParams(
                collective_id=0, has_side_effects=True, vmem_limit_bytes=60 << 20
            ),
        )(queries, stale_kv, residual_codes, scale_exponents)

    return jax.shard_map(
        per_device,
        mesh=mesh,
        in_specs=(
            P(("req", "patch"), None),
            P(None, ("req", "patch"), None),
            P(None, ("req", "patch"), None),
            P(None, ("req", "patch"), None),
        ),
        out_specs=P(("req", "patch"), None),
        check_vma=False,
    )
```

```python
import functools
import math

import jax
import jax.numpy as jnp
from jax import lax
from jax.experimental import pallas as pl
from jax.experimental.pallas import tpu as pltpu
from jax.sharding import PartitionSpec as P

HEADS = 20
HD = 128
BLOCK = 32
MESH = pl.DeviceIdType.MESH
VMEM_LIMIT = 60 << 20


def spans(n):
    return max((HEADS * d + HEADS - 1) // n - HEADS * d // n + 1 for d in range(n))


def shared_head_kernel(
    n, group, span,
    q_ref, stale_ref, codes_ref, scale_ref, out_ref,
    stale_v, codes_v, scale_v, own, kv_in, q_in, o_buf,
    in_sem, kv_send, kv_recv, q_send, q_recv, o_send, o_recv,
):
    per = HEADS // group
    blocks = n // group
    rows = q_ref.shape[0]
    req = lax.axis_index("req")
    me = lax.axis_index("patch")
    my_blk, my_pos = lax.div(me, group), lax.rem(me, group)

    def first_head(d):
        return jnp.minimum(lax.div(HEADS * d, n), HEADS - span)

    barrier = pltpu.get_barrier_semaphore()

    def greet(k, c):
        pl.semaphore_signal(
            barrier, inc=1, device_id=(req, lax.rem(me + k, n)), device_id_type=MESH
        )
        return c

    loads = [
        pltpu.make_async_copy(scale_ref, scale_v, in_sem.at[0]),
        pltpu.make_async_copy(codes_ref, codes_v, in_sem.at[1]),
        pltpu.make_async_copy(stale_ref, stale_v, in_sem.at[2]),
    ]
    for load in loads:
        load.start()
    lax.fori_loop(1, n, greet, 0)
    for load in loads:
        load.wait()

    def store(h, x, value):
        own[h, x] = value

    decode(codes_v, stale_v, scale_v, store)
    pl.semaphore_wait(barrier, n - 1)

    def kv_copy(d):
        return pltpu.make_async_remote_copy(
            src_ref=own.at[pl.ds(first_head(d), span)],
            dst_ref=kv_in.at[:, :, me],
            send_sem=kv_send.at[d],
            recv_sem=kv_recv.at[me],
            device_id=(req, d),
            device_id_type=MESH,
        )

    def send_kv(k, c):
        kv_copy(lax.rem(me + k, n)).start()
        return c

    own_kv = pltpu.make_async_copy(
        own.at[pl.ds(first_head(me), span)], kv_in.at[:, :, me], kv_recv.at[me]
    )

    def q_route(h):
        unit = h * blocks + my_blk
        d = lax.div(unit, per)
        return d, lax.rem(unit, per) * group + my_pos

    def q_lanes(ref, h):
        return ref.at[:, pl.ds(pl.multiple_of(h * HD, HD), HD)]

    def q_copy(h):
        d, slot = q_route(h)
        return pltpu.make_async_remote_copy(
            src_ref=q_lanes(q_ref, h), dst_ref=q_in.at[slot],
            send_sem=q_send.at[h], recv_sem=q_recv.at[slot],
            device_id=(req, d), device_id_type=MESH,
        )

    def q_local(h):
        d, slot = q_route(h)
        return pltpu.make_async_copy(q_lanes(q_ref, h), q_in.at[slot], q_recv.at[slot])

    def send_q(h, c):
        d, slot = q_route(h)

        @pl.when(d != me)
        def _():
            q_copy(h).start()

        @pl.when(d == me)
        def _():
            q_local(h).start()

        return c

    lax.fori_loop(0, HEADS, send_q, 0)
    lax.fori_loop(1, n, send_kv, 0)
    own_kv.start()

    def wait_q(slot, c):
        pltpu.make_async_copy(q_lanes(q_ref, 0), q_in.at[slot], q_recv.at[slot]).wait()
        return c

    def wait_kv(s, c):
        pltpu.make_async_copy(
            own.at[pl.ds(0, span)], kv_in.at[:, :, s], kv_recv.at[s]
        ).wait()
        return c

    lax.fori_loop(0, HEADS, wait_q, 0)
    lax.fori_loop(0, n, wait_kv, 0)

    def o_route(slot):
        t, i = divmod(slot, group)
        unit = me * per + t
        h = lax.div(unit, blocks)
        return h, lax.rem(unit, blocks) * group + i

    for t in range(per):
        h = lax.div(me * per + t, blocks)
        at = h - first_head(me)
        head_query = q_in[t * group:(t + 1) * group].astype(jnp.float32)
        head_query = head_query.reshape(group * rows, HD).astype(jnp.bfloat16)
        head_key = kv_in[at, 0].astype(jnp.float32).reshape(n * rows, HD).astype(jnp.bfloat16)
        head_value = kv_in[at, 1].astype(jnp.float32).reshape(n * rows, HD).astype(jnp.bfloat16)
        scores = lax.dot_general(
            head_query, head_key, (((1,), (1,)), ((), ())),
            preferred_element_type=jnp.float32,
        ) * (HD ** -0.5)
        weights = jnp.exp(scores - jnp.max(scores, axis=1, keepdims=True))
        total = jnp.sum(weights, axis=1, keepdims=True)
        summed = jnp.dot(
            weights.astype(jnp.bfloat16), head_value, preferred_element_type=jnp.float32
        )
        o_buf[t * group:(t + 1) * group] = (
            (summed / total).reshape(group, rows, HD).astype(jnp.bfloat16)
        )
        for i in range(group):
            slot = t * group + i
            h, d = o_route(slot)

            @pl.when(d != me)
            def _():
                pltpu.make_async_remote_copy(
                    src_ref=o_buf.at[slot], dst_ref=q_lanes(out_ref, h),
                    send_sem=o_send.at[slot], recv_sem=o_recv.at[h],
                    device_id=(req, d), device_id_type=MESH,
                ).start()

            @pl.when(d == me)
            def _():
                pltpu.make_async_copy(
                    o_buf.at[slot], q_lanes(out_ref, h), o_recv.at[h]
                ).start()

    def drain_kv(k, c):
        kv_copy(lax.rem(me + k, n)).wait_send()
        return c

    def drain_q(h, c):
        d, slot = q_route(h)

        @pl.when(d != me)
        def _():
            q_copy(h).wait_send()

        return c

    lax.fori_loop(1, n, drain_kv, 0)
    lax.fori_loop(0, HEADS, drain_q, 0)
    for slot in range(HEADS):
        h, d = o_route(slot)

        @pl.when(d != me)
        def _():
            pltpu.make_async_remote_copy(
                src_ref=o_buf.at[slot], dst_ref=q_lanes(out_ref, h),
                send_sem=o_send.at[slot], recv_sem=o_recv.at[h],
                device_id=(req, d), device_id_type=MESH,
            ).wait_send()

    def wait_o(h, c):
        pltpu.make_async_copy(o_buf.at[0], q_lanes(out_ref, h), o_recv.at[h]).wait()
        return c

    lax.fori_loop(0, HEADS, wait_o, 0)


def decode(codes_v, stale_v, scale_v, store):
    groups, width = HEADS * HD // BLOCK, HEADS * HD
    spread = (
        lax.shift_right_logical(lax.broadcasted_iota(jnp.int32, (groups, width), 1), 5)
        == lax.broadcasted_iota(jnp.int32, (groups, width), 0)
    ).astype(jnp.float32).astype(jnp.bfloat16)
    for x in range(2):
        power = lax.shift_left(jnp.ones_like(scale_v[x]), scale_v[x])
        power = power.astype(jnp.float32).astype(jnp.bfloat16)
        block_scale = jnp.dot(power, spread, preferred_element_type=jnp.float32)
        for h in range(HEADS):
            lanes = slice(h * HD, (h + 1) * HD)
            code = codes_v[x, :, lanes]
            exponent = lax.shift_right_logical(code, 3) & 15
            mantissa = code & 7
            whole = jnp.where(exponent > 0, mantissa + 8, mantissa)
            whole = lax.shift_left(whole, jnp.maximum(exponent - 1, 0))
            whole = jnp.where(code >= 128, -whole, whole)
            residual = whole.astype(jnp.float32) * (block_scale[:, lanes] * 2.0**-25)
            kept = stale_v[x, :, lanes].astype(jnp.float32)
            store(h, x, (kept + residual).astype(jnp.bfloat16))


def whole_head_kernel(
    n, heavy,
    q_ref, stale_ref, codes_ref, scale_ref, out_ref,
    q_v, stale_v, codes_v, scale_v, own, arrived, o_buf,
    in_sem, qkv_send, qkv_recv, o_send, o_recv,
):
    rows = q_ref.shape[0]
    base = HEADS // n
    most = arrived.shape[0]
    req = lax.axis_index("req")
    me = lax.axis_index("patch")
    order = sorted(range(1, n), key=lambda k: abs(2 * k - n))

    def partner(k):
        d = me + k
        return jnp.where(d >= n, d - n, d)

    def first_head(d):
        return sum([jnp.where(d > e, 1, 0) for e in heavy], base * d)

    def is_heavy(d):
        return sum([jnp.where(d == e, 1, 0) for e in heavy], 0 * d) > 0

    def columns(ref, h, count):
        return ref.at[:, pl.ds(pl.multiple_of(h * HD, HD), count * HD)]

    loads = [
        pltpu.make_async_copy(a, b, in_sem.at[i])
        for i, (a, b) in enumerate(
            [(scale_ref, scale_v), (codes_ref, codes_v), (stale_ref, stale_v), (q_ref, q_v)]
        )
    ]
    for load in loads:
        load.start()
    barrier = pltpu.get_barrier_semaphore()
    for k in order:
        pl.semaphore_signal(
            barrier, inc=1, device_id=(req, partner(k)), device_id_type=MESH
        )
    for load in loads:
        load.wait()

    def store(h, x, value):
        own[h, 1 + x] = value

    decode(codes_v, stale_v, scale_v, store)
    for h in range(HEADS):
        own[h, 0] = q_v[:, h * HD:(h + 1) * HD]
    pl.semaphore_wait(barrier, n - 1)

    def for_head(slot, d, run):
        if slot < base:
            run()
        elif heavy:
            pl.when(is_heavy(d))(run)

    def send(slot, k):
        d = partner(k)
        return pltpu.make_async_remote_copy(
            src_ref=own.at[first_head(d) + slot],
            dst_ref=arrived.at[slot, :, me],
            send_sem=qkv_send.at[slot, k],
            recv_sem=qkv_recv.at[slot, me],
            device_id=(req, d),
            device_id_type=MESH,
        )

    def keep(slot):
        return pltpu.make_async_copy(
            own.at[first_head(me) + slot], arrived.at[slot, :, me], qkv_recv.at[slot, me]
        )

    def landed(slot, s):
        return pltpu.make_async_copy(own.at[0], arrived.at[slot, :, s], qkv_recv.at[slot, s])

    for k in order:
        for slot in range(most):
            for_head(slot, partner(k), lambda: send(slot, k).start())
    for slot in range(most):
        for_head(slot, me, lambda: keep(slot).start())

    def attend(slot):
        for s in range(n):
            landed(slot, s).wait()

        def flat(x):
            return arrived[slot, x].astype(jnp.float32).reshape(n * rows, HD).astype(jnp.bfloat16)

        scores = lax.dot_general(
            flat(0), flat(1), (((1,), (1,)), ((), ())), preferred_element_type=jnp.float32
        )
        top = jnp.max(scores, axis=1, keepdims=True)
        weights = jnp.exp((scores - top) * (HD ** -0.5))
        total = jnp.sum(weights, axis=1, keepdims=True)
        summed = jnp.dot(
            weights.astype(jnp.bfloat16), flat(2), preferred_element_type=jnp.float32
        )
        result = (summed / total).reshape(n, rows, HD).astype(jnp.bfloat16)
        o_buf[:, :, slot * HD:(slot + 1) * HD] = result

    for slot in range(most):
        for_head(slot, me, lambda: attend(slot))

    def give(k, count):
        return pltpu.make_async_remote_copy(
            src_ref=columns(o_buf.at[partner(k)], 0, count),
            dst_ref=columns(out_ref, first_head(me), count),
            send_sem=o_send.at[k],
            recv_sem=o_recv.at[me],
            device_id=(req, partner(k)),
            device_id_type=MESH,
        )

    def give_all(count):
        for k in order:
            give(k, count).start()
        pltpu.make_async_copy(
            columns(o_buf.at[me], 0, count),
            columns(out_ref, first_head(me), count),
            o_recv.at[me],
        ).start()

    def drain_all(count):
        for k in order:
            give(k, count).wait_send()

    def by_load(run):
        if heavy:
            pl.when(is_heavy(me))(lambda: run(base + 1))
            pl.when(jnp.logical_not(is_heavy(me)))(lambda: run(base))
        else:
            run(base)

    by_load(give_all)
    for k in order:
        for slot in range(most):
            for_head(slot, partner(k), lambda: send(slot, k).wait_send())
    for d in range(n):
        count = base + (d in heavy)
        pltpu.make_async_copy(
            columns(o_buf.at[0], 0, count), columns(out_ref, 0, count), o_recv.at[d]
        ).wait()
    by_load(drain_all)


def whole_heads(n, rows, specs, operands):
    extra = HEADS % n
    step = n // extra if extra else 1
    heavy = tuple(j * step + (j % 2) * (step // 2) for j in range(extra))
    most = HEADS // n + bool(extra)
    queries, stale_kv, residual_codes, scale_exponents = operands
    bf16, dma = jnp.bfloat16, pltpu.SemaphoreType.DMA
    return pl.pallas_call(
        functools.partial(whole_head_kernel, n, heavy),
        out_shape=jax.ShapeDtypeStruct(queries.shape, bf16),
        scratch_shapes=[
            pltpu.VMEM(queries.shape, bf16),
            pltpu.VMEM(stale_kv.shape, bf16),
            pltpu.VMEM(residual_codes.shape, jnp.int32),
            pltpu.VMEM(scale_exponents.shape, jnp.int32),
            pltpu.VMEM((HEADS, 3, rows, HD), bf16),
            pltpu.VMEM((most, 3, n, rows, HD), bf16),
            pltpu.VMEM((n, rows, most * HD), bf16),
            dma((4,)),
            dma((most, n)), dma((most, n)),
            dma((n,)), dma((n,)),
        ],
        compiler_params=pltpu.CompilerParams(
            collective_id=0, has_side_effects=True, vmem_limit_bytes=VMEM_LIMIT
        ),
        **specs,
    )(*operands)


def solution(mesh):
    n = mesh.shape["patch"]
    group = math.gcd(HEADS, n)
    span = spans(n)

    def per_device(queries, stale_kv, residual_codes, scale_exponents):
        rows = queries.shape[0]
        specs = dict(
            in_specs=[pl.BlockSpec(memory_space=pltpu.HBM)] * 4,
            out_specs=pl.BlockSpec(memory_space=pl.ANY),
        )
        operands = (queries, stale_kv, residual_codes, scale_exponents)
        if n <= HEADS:
            return whole_heads(n, rows, specs, operands)
        bf16, dma = jnp.bfloat16, pltpu.SemaphoreType.DMA
        return pl.pallas_call(
            functools.partial(shared_head_kernel, n, group, span),
            out_shape=jax.ShapeDtypeStruct(queries.shape, bf16),
            scratch_shapes=[
                pltpu.VMEM(stale_kv.shape, bf16),
                pltpu.VMEM(residual_codes.shape, jnp.int32),
                pltpu.VMEM(scale_exponents.shape, jnp.int32),
                pltpu.VMEM((HEADS, 2, rows, HD), bf16),
                pltpu.VMEM((span, 2, n, rows, HD), bf16),
                pltpu.VMEM((HEADS, rows, HD), bf16),
                pltpu.VMEM((HEADS, rows, HD), bf16),
                dma((3,)),
                dma((n,)), dma((n,)),
                dma((HEADS,)), dma((HEADS,)),
                dma((HEADS,)), dma((HEADS,)),
            ],
            compiler_params=pltpu.CompilerParams(
                collective_id=0, has_side_effects=True, vmem_limit_bytes=VMEM_LIMIT
            ),
            **specs,
        )(*operands)

    return jax.shard_map(
        per_device,
        mesh=mesh,
        in_specs=(
            P(("req", "patch"), None),
            P(None, ("req", "patch"), None),
            P(None, ("req", "patch"), None),
            P(None, ("req", "patch"), None),
        ),
        out_specs=P(("req", "patch"), None),
        check_vma=False,
    )
```

```python
import functools
import math

import jax
import jax.numpy as jnp
from jax import lax
from jax.experimental import pallas as pl
from jax.experimental.pallas import tpu as pltpu
from jax.sharding import PartitionSpec as P

HEADS = 20
HD = 128
BLOCK = 32
MESH = pl.DeviceIdType.MESH
VMEM_LIMIT = 60 << 20


def spans(n):
    return max((HEADS * d + HEADS - 1) // n - HEADS * d // n + 1 for d in range(n))


def shared_head_kernel(
    n, group, span,
    q_ref, stale_ref, codes_ref, scale_ref, out_ref,
    stale_v, codes_v, scale_v, own, kv_in, q_in, o_buf,
    in_sem, kv_send, kv_recv, q_send, q_recv, o_send, o_recv,
):
    per = HEADS // group
    blocks = n // group
    rows = q_ref.shape[0]
    req = lax.axis_index("req")
    me = lax.axis_index("patch")
    my_blk, my_pos = lax.div(me, group), lax.rem(me, group)

    def first_head(d):
        return jnp.minimum(lax.div(HEADS * d, n), HEADS - span)

    barrier = pltpu.get_barrier_semaphore()

    def greet(k, c):
        pl.semaphore_signal(
            barrier, inc=1, device_id=(req, lax.rem(me + k, n)), device_id_type=MESH
        )
        return c

    loads = [
        pltpu.make_async_copy(scale_ref, scale_v, in_sem.at[0]),
        pltpu.make_async_copy(codes_ref, codes_v, in_sem.at[1]),
        pltpu.make_async_copy(stale_ref, stale_v, in_sem.at[2]),
    ]
    for load in loads:
        load.start()
    lax.fori_loop(1, n, greet, 0)
    for load in loads:
        load.wait()

    def store(h, x, value):
        own[h, x] = value

    decode(codes_v, stale_v, scale_v, store)
    pl.semaphore_wait(barrier, n - 1)

    def kv_copy(d):
        return pltpu.make_async_remote_copy(
            src_ref=own.at[pl.ds(first_head(d), span)],
            dst_ref=kv_in.at[:, :, me],
            send_sem=kv_send.at[d],
            recv_sem=kv_recv.at[me],
            device_id=(req, d),
            device_id_type=MESH,
        )

    def send_kv(k, c):
        kv_copy(lax.rem(me + k, n)).start()
        return c

    own_kv = pltpu.make_async_copy(
        own.at[pl.ds(first_head(me), span)], kv_in.at[:, :, me], kv_recv.at[me]
    )

    def q_route(h):
        unit = h * blocks + my_blk
        d = lax.div(unit, per)
        return d, lax.rem(unit, per) * group + my_pos

    def q_lanes(ref, h):
        return ref.at[:, pl.ds(pl.multiple_of(h * HD, HD), HD)]

    def q_copy(h):
        d, slot = q_route(h)
        return pltpu.make_async_remote_copy(
            src_ref=q_lanes(q_ref, h), dst_ref=q_in.at[slot],
            send_sem=q_send.at[h], recv_sem=q_recv.at[slot],
            device_id=(req, d), device_id_type=MESH,
        )

    def q_local(h):
        d, slot = q_route(h)
        return pltpu.make_async_copy(q_lanes(q_ref, h), q_in.at[slot], q_recv.at[slot])

    def send_q(h, c):
        d, slot = q_route(h)

        @pl.when(d != me)
        def _():
            q_copy(h).start()

        @pl.when(d == me)
        def _():
            q_local(h).start()

        return c

    lax.fori_loop(0, HEADS, send_q, 0)
    lax.fori_loop(1, n, send_kv, 0)
    own_kv.start()

    def wait_q(slot, c):
        pltpu.make_async_copy(q_lanes(q_ref, 0), q_in.at[slot], q_recv.at[slot]).wait()
        return c

    def wait_kv(s, c):
        pltpu.make_async_copy(
            own.at[pl.ds(0, span)], kv_in.at[:, :, s], kv_recv.at[s]
        ).wait()
        return c

    lax.fori_loop(0, HEADS, wait_q, 0)
    lax.fori_loop(0, n, wait_kv, 0)

    def o_route(slot):
        t, i = divmod(slot, group)
        unit = me * per + t
        h = lax.div(unit, blocks)
        return h, lax.rem(unit, blocks) * group + i

    for t in range(per):
        h = lax.div(me * per + t, blocks)
        at = h - first_head(me)
        head_query = q_in[t * group:(t + 1) * group].astype(jnp.float32)
        head_query = head_query.reshape(group * rows, HD).astype(jnp.bfloat16)
        head_key = kv_in[at, 0].astype(jnp.float32).reshape(n * rows, HD).astype(jnp.bfloat16)
        head_value = kv_in[at, 1].astype(jnp.float32).reshape(n * rows, HD).astype(jnp.bfloat16)
        scores = lax.dot_general(
            head_query, head_key, (((1,), (1,)), ((), ())),
            preferred_element_type=jnp.float32,
        ) * (HD ** -0.5)
        weights = jnp.exp(scores - jnp.max(scores, axis=1, keepdims=True))
        total = jnp.sum(weights, axis=1, keepdims=True)
        summed = jnp.dot(
            weights.astype(jnp.bfloat16), head_value, preferred_element_type=jnp.float32
        )
        o_buf[t * group:(t + 1) * group] = (
            (summed / total).reshape(group, rows, HD).astype(jnp.bfloat16)
        )
        for i in range(group):
            slot = t * group + i
            h, d = o_route(slot)

            @pl.when(d != me)
            def _():
                pltpu.make_async_remote_copy(
                    src_ref=o_buf.at[slot], dst_ref=q_lanes(out_ref, h),
                    send_sem=o_send.at[slot], recv_sem=o_recv.at[h],
                    device_id=(req, d), device_id_type=MESH,
                ).start()

            @pl.when(d == me)
            def _():
                pltpu.make_async_copy(
                    o_buf.at[slot], q_lanes(out_ref, h), o_recv.at[h]
                ).start()

    def drain_kv(k, c):
        kv_copy(lax.rem(me + k, n)).wait_send()
        return c

    def drain_q(h, c):
        d, slot = q_route(h)

        @pl.when(d != me)
        def _():
            q_copy(h).wait_send()

        return c

    lax.fori_loop(1, n, drain_kv, 0)
    lax.fori_loop(0, HEADS, drain_q, 0)
    for slot in range(HEADS):
        h, d = o_route(slot)

        @pl.when(d != me)
        def _():
            pltpu.make_async_remote_copy(
                src_ref=o_buf.at[slot], dst_ref=q_lanes(out_ref, h),
                send_sem=o_send.at[slot], recv_sem=o_recv.at[h],
                device_id=(req, d), device_id_type=MESH,
            ).wait_send()

    def wait_o(h, c):
        pltpu.make_async_copy(o_buf.at[0], q_lanes(out_ref, h), o_recv.at[h]).wait()
        return c

    lax.fori_loop(0, HEADS, wait_o, 0)


def decode(codes_v, stale_v, scale_v, store):
    groups, width = HEADS * HD // BLOCK, HEADS * HD
    spread = (
        lax.shift_right_logical(lax.broadcasted_iota(jnp.int32, (groups, width), 1), 5)
        == lax.broadcasted_iota(jnp.int32, (groups, width), 0)
    ).astype(jnp.float32).astype(jnp.bfloat16)
    for x in range(2):
        power = lax.shift_left(jnp.ones_like(scale_v[x]), scale_v[x])
        power = power.astype(jnp.float32).astype(jnp.bfloat16)
        block_scale = jnp.dot(power, spread, preferred_element_type=jnp.float32)
        for h in range(HEADS):
            lanes = slice(h * HD, (h + 1) * HD)
            code = codes_v[x, :, lanes]
            exponent = lax.shift_right_logical(code, 3) & 15
            mantissa = code & 7
            whole = jnp.where(exponent > 0, mantissa + 8, mantissa)
            whole = lax.shift_left(whole, jnp.maximum(exponent - 1, 0))
            whole = jnp.where(code >= 128, -whole, whole)
            residual = whole.astype(jnp.float32) * (block_scale[:, lanes] * 2.0**-25)
            kept = stale_v[x, :, lanes].astype(jnp.float32)
            store(h, x, (kept + residual).astype(jnp.bfloat16))


def whole_head_kernel(
    n, heavy,
    q_ref, stale_ref, codes_ref, scale_ref, out_ref,
    q_v, stale_v, codes_v, scale_v, own, arrived, o_buf,
    in_sem, qkv_send, qkv_recv, o_send, o_recv,
):
    rows = q_ref.shape[0]
    base = HEADS // n
    most = arrived.shape[0]
    req = lax.axis_index("req")
    me = lax.axis_index("patch")
    order = sorted(range(1, n), key=lambda k: -abs(2 * k - n))

    def partner(k):
        d = me + k
        return jnp.where(d >= n, d - n, d)

    def first_head(d):
        return sum([jnp.where(d > e, 1, 0) for e in heavy], base * d)

    def is_heavy(d):
        return sum([jnp.where(d == e, 1, 0) for e in heavy], 0 * d) > 0

    def columns(ref, h, count):
        return ref.at[:, pl.ds(pl.multiple_of(h * HD, HD), count * HD)]

    loads = [
        pltpu.make_async_copy(a, b, in_sem.at[i])
        for i, (a, b) in enumerate(
            [(scale_ref, scale_v), (codes_ref, codes_v), (stale_ref, stale_v), (q_ref, q_v)]
        )
    ]
    for load in loads:
        load.start()
    barrier = pltpu.get_barrier_semaphore()
    for k in order:
        pl.semaphore_signal(
            barrier, inc=1, device_id=(req, partner(k)), device_id_type=MESH
        )
    for load in loads:
        load.wait()

    def store(h, x, value):
        own[h, 1 + x] = value

    decode(codes_v, stale_v, scale_v, store)
    for h in range(HEADS):
        own[h, 0] = q_v[:, h * HD:(h + 1) * HD]
    pl.semaphore_wait(barrier, n - 1)

    def for_head(slot, d, run):
        if slot < base:
            run()
        elif heavy:
            pl.when(is_heavy(d))(run)

    def send(slot, k):
        d = partner(k)
        return pltpu.make_async_remote_copy(
            src_ref=own.at[first_head(d) + slot],
            dst_ref=arrived.at[slot, :, me],
            send_sem=qkv_send.at[slot, k],
            recv_sem=qkv_recv.at[slot, me],
            device_id=(req, d),
            device_id_type=MESH,
        )

    def keep(slot):
        return pltpu.make_async_copy(
            own.at[first_head(me) + slot], arrived.at[slot, :, me], qkv_recv.at[slot, me]
        )

    def landed(slot, s):
        return pltpu.make_async_copy(own.at[0], arrived.at[slot, :, s], qkv_recv.at[slot, s])

    for k in order:
        for slot in range(most):
            for_head(slot, partner(k), lambda: send(slot, k).start())
    for slot in range(most):
        for_head(slot, me, lambda: keep(slot).start())

    def attend(slot):
        for s in range(n):
            landed(slot, s).wait()

        def flat(x):
            return arrived[slot, x].astype(jnp.float32).reshape(n * rows, HD).astype(jnp.bfloat16)

        scores = lax.dot_general(
            flat(0), flat(1), (((1,), (1,)), ((), ())), preferred_element_type=jnp.float32
        )
        top = jnp.max(scores, axis=1, keepdims=True)
        weights = jnp.exp((scores - top) * (HD ** -0.5))
        total = jnp.sum(weights, axis=1, keepdims=True)
        summed = jnp.dot(
            weights.astype(jnp.bfloat16), flat(2), preferred_element_type=jnp.float32
        )
        result = (summed / total).reshape(n, rows, HD).astype(jnp.bfloat16)
        o_buf[:, :, slot * HD:(slot + 1) * HD] = result

    for slot in range(most):
        for_head(slot, me, lambda: attend(slot))

    def give(k, count):
        return pltpu.make_async_remote_copy(
            src_ref=columns(o_buf.at[partner(k)], 0, count),
            dst_ref=columns(out_ref, first_head(me), count),
            send_sem=o_send.at[k],
            recv_sem=o_recv.at[me],
            device_id=(req, partner(k)),
            device_id_type=MESH,
        )

    def give_all(count):
        for k in order:
            give(k, count).start()
        pltpu.make_async_copy(
            columns(o_buf.at[me], 0, count),
            columns(out_ref, first_head(me), count),
            o_recv.at[me],
        ).start()

    def drain_all(count):
        for k in order:
            give(k, count).wait_send()

    def by_load(run):
        if heavy:
            pl.when(is_heavy(me))(lambda: run(base + 1))
            pl.when(jnp.logical_not(is_heavy(me)))(lambda: run(base))
        else:
            run(base)

    by_load(give_all)
    for k in order:
        for slot in range(most):
            for_head(slot, partner(k), lambda: send(slot, k).wait_send())
    for d in range(n):
        count = base + (d in heavy)
        pltpu.make_async_copy(
            columns(o_buf.at[0], 0, count), columns(out_ref, 0, count), o_recv.at[d]
        ).wait()
    by_load(drain_all)


def whole_heads(n, rows, specs, operands):
    extra = HEADS % n
    step = n // extra if extra else 1
    heavy = tuple(j * step + (j % 2) * (step // 2) for j in range(extra))
    most = HEADS // n + bool(extra)
    queries, stale_kv, residual_codes, scale_exponents = operands
    bf16, dma = jnp.bfloat16, pltpu.SemaphoreType.DMA
    return pl.pallas_call(
        functools.partial(whole_head_kernel, n, heavy),
        out_shape=jax.ShapeDtypeStruct(queries.shape, bf16),
        scratch_shapes=[
            pltpu.VMEM(queries.shape, bf16),
            pltpu.VMEM(stale_kv.shape, bf16),
            pltpu.VMEM(residual_codes.shape, jnp.int32),
            pltpu.VMEM(scale_exponents.shape, jnp.int32),
            pltpu.VMEM((HEADS, 3, rows, HD), bf16),
            pltpu.VMEM((most, 3, n, rows, HD), bf16),
            pltpu.VMEM((n, rows, most * HD), bf16),
            dma((4,)),
            dma((most, n)), dma((most, n)),
            dma((n,)), dma((n,)),
        ],
        compiler_params=pltpu.CompilerParams(
            collective_id=0, has_side_effects=True, vmem_limit_bytes=VMEM_LIMIT
        ),
        **specs,
    )(*operands)


def solution(mesh):
    n = mesh.shape["patch"]
    group = math.gcd(HEADS, n)
    span = spans(n)

    def per_device(queries, stale_kv, residual_codes, scale_exponents):
        rows = queries.shape[0]
        specs = dict(
            in_specs=[pl.BlockSpec(memory_space=pltpu.HBM)] * 4,
            out_specs=pl.BlockSpec(memory_space=pl.ANY),
        )
        operands = (queries, stale_kv, residual_codes, scale_exponents)
        if n <= HEADS:
            return whole_heads(n, rows, specs, operands)
        bf16, dma = jnp.bfloat16, pltpu.SemaphoreType.DMA
        return pl.pallas_call(
            functools.partial(shared_head_kernel, n, group, span),
            out_shape=jax.ShapeDtypeStruct(queries.shape, bf16),
            scratch_shapes=[
                pltpu.VMEM(stale_kv.shape, bf16),
                pltpu.VMEM(residual_codes.shape, jnp.int32),
                pltpu.VMEM(scale_exponents.shape, jnp.int32),
                pltpu.VMEM((HEADS, 2, rows, HD), bf16),
                pltpu.VMEM((span, 2, n, rows, HD), bf16),
                pltpu.VMEM((HEADS, rows, HD), bf16),
                pltpu.VMEM((HEADS, rows, HD), bf16),
                dma((3,)),
                dma((n,)), dma((n,)),
                dma((HEADS,)), dma((HEADS,)),
                dma((HEADS,)), dma((HEADS,)),
            ],
            compiler_params=pltpu.CompilerParams(
                collective_id=0, has_side_effects=True, vmem_limit_bytes=VMEM_LIMIT
            ),
            **specs,
        )(*operands)

    return jax.shard_map(
        per_device,
        mesh=mesh,
        in_specs=(
            P(("req", "patch"), None),
            P(None, ("req", "patch"), None),
            P(None, ("req", "patch"), None),
            P(None, ("req", "patch"), None),
        ),
        out_specs=P(("req", "patch"), None),
        check_vma=False,
    )
```
